32 devices in a mesh: tok: 4 (over z), blk: 8 (over y, x, core).
Axes of the slice: x: 2, y: 2, z: 4, core: 2. Of those that a mesh axis runs over, the one named last changes fastest.
Arguments:
- acts: bfloat16 [512, 8192], P('tok', 'blk'), may hold values from -35 to 35
- out_grad: bfloat16 [512, 29568], P(('tok', 'blk')), may hold values from -0.12 to 0.12
- kept_ids: int32 [8, 16], replicated, may hold values from 0 to 14783, as said below
- cand_ids: int32 [8, 48], replicated, may hold values from 0 to 14783, as said below
Outputs:
- kept_grad: bfloat16 [8, 16, 128, 128], P('blk', 'tok')
- cand_score: float32 [8, 48], P('blk', 'tok')
The draws below stay inside these ranges and needn't reach their ends.
Inputs may be any that keep to these rules, and one draw needn't show every extreme that they name: `kept_ids`: within one owner's kept and candidate blocks every block id appears once; one owner's blocks use at most 58 distinct block columns, exactly 58 for some owner, and no block column is used by two owners. `cand_ids`: numbered and owned as the kept blocks, and distinct from them.
All inputs are finite; a program needn't handle non-finite values.
Results may differ from the reference program's by a relative error of at most 0.001.
Values may be sent and summed in bfloat16 or wider, within the bound.
No kernel may reach another device: no remote copies, remote signals or barrier semaphores. Data moves between devices by JAX's collectives and lax.ppermute only.
A program may use at most 64 MiB of HBM per device.

```python
import math
import jax
import jax.numpy as jnp
from jax import lax

D = 8192
F = 29568
BLOCK = 128
TOK_DEV = 128
KS = 16
CS = 48
TOKENS = 512
NRB = 64
NCB = 231
BLOCK_HOLDERS = 8
MC = 58


def owner_table(key):
    key_cols, key_owner = jax.random.split(key)
    col_order = jax.random.permutation(key_cols, NCB)
    owner_order = jax.random.permutation(key_owner, BLOCK_HOLDERS)
    position = jnp.arange(NCB)
    first = MC + 2 * (BLOCK_HOLDERS - 1)
    slot = jnp.where(position < MC, 0, jnp.where(position < first, 1 + (position - MC) // 2, 1 + (position - first) % (BLOCK_HOLDERS - 1)))
    owner_at = owner_order[slot]
    return jnp.zeros((NCB,), jnp.int32).at[col_order].set(owner_at.astype(jnp.int32))


def block_lists(key):
    col_owner = owner_table(jax.random.fold_in(key, 1))
    ranking_score = jax.random.fold_in(key, 2)
    key_row = jax.random.fold_in(key, 3)
    grand_total = NRB * NCB
    entry_index = jnp.arange(grand_total)
    block_column_index = entry_index % NCB
    block_row_index = entry_index // NCB
    selected_row = jax.random.randint(key_row, (NCB,), 0, NRB)
    extra_score = jnp.where(block_row_index == selected_row[block_column_index], 1 << 30, 0)
    base_offset = jax.random.randint(ranking_score, (BLOCK_HOLDERS, grand_total), 0, 32768) * grand_total + entry_index[None, :] + extra_score[None, :]
    owned = col_owner[block_column_index][None, :] == jnp.arange(BLOCK_HOLDERS)[:, None]
    scores = jnp.where(owned, base_offset, -1 - entry_index[None, :])
    chosen = jax.lax.top_k(scores, KS + CS)[1].astype(jnp.int32)
    return chosen


def draw_kept_ids(key, part):
    return block_lists(key)[:, :KS]


def draw_cand_ids(key, part):
    return block_lists(key)[:, KS:]


def feature_scales(key, count, low, ratio):
    key_block, key_rough = jax.random.split(key)
    block_scale = low * jnp.exp(math.log(ratio) * jax.random.uniform(key_block, (count // BLOCK, 1)))
    rough = jnp.exp(math.log(2.0) * (jax.random.uniform(key_rough, (count // BLOCK, BLOCK)) - 0.5))
    return (block_scale * rough).reshape(count)


def draw_acts(key, part):
    key_val, key_scale = jax.random.split(key)
    values = jnp.clip(jax.random.normal(key_val, (TOKENS, D)), -5.0, 5.0)
    scales = feature_scales(key_scale, D, 0.5, 10.0)
    return (values * scales[None, :]).astype(jnp.bfloat16)


def draw_out_grad(key, part):
    key_val, key_scale = jax.random.split(key)
    values = jnp.clip(jax.random.normal(key_val, (TOKENS, F)), -5.0, 5.0)
    scales = feature_scales(key_scale, F, 0.7071, 2.0)
    return (values * scales[None, :] * 0.011).astype(jnp.bfloat16)


def setup_inputs(seed: int = 0) -> dict:
    streams_of = jax.random.split(jax.random.key(seed), 5)
    acts = draw_acts(jax.random.fold_in(streams_of[4], 71), 0)
    out_grad = draw_out_grad(jax.random.fold_in(streams_of[4], 71), 0)
    kept_ids = draw_kept_ids(jax.random.fold_in(streams_of[4], 71), 0)
    cand_ids = draw_cand_ids(jax.random.fold_in(streams_of[4], 71), 0)
    return {"acts": acts, "out_grad": out_grad, "kept_ids": kept_ids, "cand_ids": cand_ids}


def block_gradient(acts3, grad3, block_id):
    row = (block_id // NCB).astype(jnp.int32)
    col = (block_id % NCB).astype(jnp.int32)
    left = lax.dynamic_slice_in_dim(acts3, row * BLOCK, BLOCK, 2).astype(jnp.float32)
    right = lax.dynamic_slice_in_dim(grad3, col * BLOCK, BLOCK, 2).astype(jnp.float32)
    partial_value = jnp.einsum('gti,gtj->gij', left, right)
    return lax.optimization_barrier(jnp.sum(partial_value, axis=0))

def reference(acts, out_grad, kept_ids, cand_ids):
    groups = acts.shape[0] // TOK_DEV
    acts3 = acts.reshape(groups, TOK_DEV, D)
    grad3 = out_grad.reshape(groups, TOK_DEV, F)

    def one_block(block_id):
        return block_gradient(acts3, grad3, block_id)
    kept_blocks = lax.map(one_block, kept_ids.reshape(-1))
    cand_blocks = lax.map(one_block, cand_ids.reshape(-1))
    kept_grad = kept_blocks.astype(jnp.bfloat16).reshape(BLOCK_HOLDERS, KS, BLOCK, BLOCK)
    norms = jnp.sqrt(lax.optimization_barrier(jnp.sum(cand_blocks * cand_blocks, axis=(1, 2))))
    peak = jnp.max(norms)
    cand_score = (norms / (peak + 1e-06)).reshape(BLOCK_HOLDERS, CS)
    return (kept_grad, cand_score)
```

```python
import functools

import jax
import jax.numpy as jnp
from jax import lax
from jax.experimental import pallas as pl
from jax.experimental.pallas import tpu as pltpu
from jax.sharding import PartitionSpec as P

BLOCK = 128
TILE_ROWS = 16
VMEM_LIMIT = 40 * 1024 * 1024
ANY = pl.BlockSpec(memory_space=pl.ANY)
VMEM = pl.BlockSpec(memory_space=pltpu.VMEM)
SMEM = pl.BlockSpec(memory_space=pltpu.SMEM)


def swap(x, axis, mask):
    size = lax.axis_size(axis)
    return lax.ppermute(x, axis, [(i, i ^ mask) for i in range(size)])


def transpose_kernel(src, dst):
    for row in range(src.shape[1] // BLOCK):
        here = pl.ds(row * BLOCK, BLOCK)
        dst[here, :] = src[:, here].T


def transpose_acts(acts):
    tokens, width = acts.shape
    return pl.pallas_call(
        transpose_kernel,
        out_shape=jax.ShapeDtypeStruct((width, tokens), acts.dtype),
        in_specs=[VMEM],
        out_specs=VMEM,
        compiler_params=pltpu.CompilerParams(vmem_limit_bytes=VMEM_LIMIT),
    )(acts)


def gather_kernel(owners, chunks, pos, cols, grad, *outs):
    rows = grad.shape[0]
    me = pos[0]
    for which, slots in enumerate(chunks):
        for peer in range(owners):
            out = outs[which * owners + peer]
            dest = me ^ peer
            for k, slot in enumerate(slots):
                start = pl.multiple_of(cols[dest, slot] * BLOCK, BLOCK)
                out[k] = grad[:, pl.ds(start, BLOCK)]


def gather_columns(out_grad, cols, pos, owners, chunks):
    rows = out_grad.shape[0]
    if rows % TILE_ROWS:
        grad3 = out_grad.reshape(rows, -1, BLOCK)
        return [
            jnp.swapaxes(jnp.take(grad3, cols[pos[0] ^ peer][jnp.array(slots)], axis=1), 0, 1)
            for slots in chunks
            for peer in range(owners)
        ]
    return pl.pallas_call(
        functools.partial(gather_kernel, owners, chunks),
        out_shape=[
            jax.ShapeDtypeStruct((len(slots), rows, BLOCK), out_grad.dtype)
            for slots in chunks
            for _ in range(owners)
        ],
        in_specs=[SMEM, SMEM, VMEM],
        out_specs=[VMEM] * (owners * len(chunks)),
        compiler_params=pltpu.CompilerParams(vmem_limit_bytes=VMEM_LIMIT),
    )(pos, cols, out_grad)


def product_kernel(owners, pieces, toks, share, first, pos, rows, *refs):
    acts = refs[:owners]
    grads = refs[owners : owners + pieces]
    outs = refs[owners + pieces : owners + pieces + toks]
    acts_all, grad_all, sem = refs[owners + pieces + toks :]
    me, tok = pos[0], pos[1]
    width = acts[0].shape[0]
    part = grads[0].shape[1]
    copies = []
    for peer in range(owners):
        src = me ^ peer
        copies.append(
            pltpu.make_async_copy(
                acts[peer],
                acts_all.at[pl.ds(pl.multiple_of(src * width, width), width)],
                sem.at[0, peer],
            )
        )
    for peer in range(pieces):
        src = me ^ peer if pieces > 1 else 0
        copies.append(
            pltpu.make_async_copy(
                grads[peer],
                grad_all.at[:, pl.ds(pl.multiple_of(src * part, part), part)],
                sem.at[1, peer],
            )
        )
    for copy in copies:
        copy.start()
    for copy in copies:
        copy.wait()
    for peer in range(toks):
        unit = tok ^ peer
        for k in range(share):
            slot = unit * share + k
            row = rows[first(unit) + k]
            left = acts_all[pl.ds(pl.multiple_of(row * BLOCK, BLOCK), BLOCK), :]
            prod = jnp.dot(left, grad_all[slot], preferred_element_type=jnp.float32)
            outs[peer][k] = prod.astype(outs[peer].dtype)


def products(acts, grads, rows, pos, toks, share, first, dtype):
    owners = len(acts)
    slots, part, _ = grads[0].shape
    tokens = acts[0].shape[1]
    if part % TILE_ROWS:
        order = pos[0] ^ jnp.arange(owners)
        whole = jnp.swapaxes(jnp.take(jnp.stack(grads), order, axis=0), 0, 1)
        grads = [whole.reshape(slots, tokens, BLOCK)]
    return pl.pallas_call(
        functools.partial(product_kernel, owners, len(grads), toks, share, first),
        out_shape=[
            jax.ShapeDtypeStruct((share, BLOCK, BLOCK), jnp.float32 if peer == 0 else dtype)
            for peer in range(toks)
        ],
        in_specs=[SMEM, SMEM] + [ANY] * (owners + len(grads)),
        out_specs=[VMEM] * toks,
        scratch_shapes=[
            pltpu.VMEM((owners * acts[0].shape[0], tokens), acts[0].dtype),
            pltpu.VMEM((slots, tokens, BLOCK), grads[0].dtype),
            pltpu.SemaphoreType.DMA((2, owners)),
        ],
        compiler_params=pltpu.CompilerParams(vmem_limit_bytes=VMEM_LIMIT),
    )(pos, rows, *acts, *grads)


def norm_kernel(counts, toks, *refs):
    norms, peak = refs[-2:]
    norms[...] = jnp.zeros_like(norms)
    at = 0
    for which, count in enumerate(counts):
        parts = refs[which * toks : (which + 1) * toks]
        for k in range(count):
            total = parts[0][k]
            for other in parts[1:]:
                total = total + other[k].astype(jnp.float32)
            norms[at : at + 1, :] = jnp.sum(total * total, axis=0, keepdims=True)
            at += 1
    each = jnp.sqrt(jnp.sum(norms[...], axis=1, keepdims=True))
    norms[...] = jnp.broadcast_to(each, norms.shape)
    peak[...] = jnp.broadcast_to(jnp.max(each, axis=0, keepdims=True), peak.shape)


def block_norms(parts, counts):
    toks = len(parts[0])
    height = -(-sum(counts) // 8) * 8
    return pl.pallas_call(
        functools.partial(norm_kernel, counts, toks),
        out_shape=[
            jax.ShapeDtypeStruct((height, BLOCK), jnp.float32),
            jax.ShapeDtypeStruct((8, BLOCK), jnp.float32),
        ],
        in_specs=[VMEM] * (toks * len(counts)),
        out_specs=[VMEM] * 2,
        compiler_params=pltpu.CompilerParams(vmem_limit_bytes=VMEM_LIMIT),
    )(*[x for chunk in parts for x in chunk])


def kept_kernel(*refs):
    total = refs[0][...]
    for other in refs[1:-1]:
        total = total + other[...]
    refs[-1][0] = total.astype(refs[-1].dtype)


def kept_sum(parts):
    return pl.pallas_call(
        kept_kernel,
        out_shape=jax.ShapeDtypeStruct((1,) + parts[0].shape, jnp.bfloat16),
        in_specs=[VMEM] * len(parts),
        out_specs=VMEM,
        compiler_params=pltpu.CompilerParams(vmem_limit_bytes=VMEM_LIMIT),
    )(*parts)


def global_peak(peak):
    mask = 1
    while mask < lax.axis_size("blk"):
        peak = jnp.maximum(peak, swap(peak, "blk", mask))
        mask *= 2
    mask = 1
    while mask < lax.axis_size("tok"):
        peak = jnp.maximum(peak, swap(peak, "tok", mask))
        mask *= 2
    return peak


def local(acts, out_grad, kept_ids, cand_ids):
    owners = lax.axis_size("blk")
    toks = lax.axis_size("tok")
    me = lax.axis_index("blk")
    tok = lax.axis_index("tok")
    pos = jnp.stack([me, tok]).astype(jnp.int32)
    ncols = out_grad.shape[1] // BLOCK
    ks = kept_ids.shape[1]
    cs = cand_ids.shape[1]
    kept_share, cand_share = ks // toks, cs // toks
    ids = jnp.concatenate([kept_ids, cand_ids], axis=1)
    cols = ids % ncols
    rows = lax.dynamic_index_in_dim(ids, me, 0, keepdims=False) // ncols

    acts_t = transpose_acts(acts)
    half = cand_share // 2
    bounds = [(0, half), (half, cand_share)]
    cand_chunks = [
        [ks + unit * cand_share + k for unit in range(toks) for k in range(lo, hi)]
        for lo, hi in bounds
    ]
    chunks = cand_chunks + [list(range(ks))]
    gathered = gather_columns(out_grad, cols, pos, owners, chunks)

    pieces = [None] * owners
    pieces[0] = acts_t
    for peer in range(2, owners, 2):
        pieces[peer] = swap(acts_t, "blk", peer)
    for peer in range(0, owners, 2):
        pieces[peer + 1] = swap(pieces[peer], "blk", 1)

    incoming = []
    for which in range(len(chunks)):
        mine = gathered[which * owners : (which + 1) * owners]
        incoming.append([mine[0]] + [swap(mine[p], "blk", p) for p in range(1, owners)])

    cand_parts = []
    for which, (lo, hi) in enumerate(bounds):
        first = lambda unit, lo=lo: ks + unit * cand_share + lo
        part = products(
            pieces, incoming[which], rows, pos, toks, hi - lo, first, jnp.bfloat16
        )
        cand_parts.append([part[0]] + [swap(part[p], "tok", p) for p in range(1, toks)])
    part = products(
        pieces,
        incoming[-1],
        rows,
        pos,
        toks,
        kept_share,
        lambda unit: unit * kept_share,
        jnp.float32,
    )
    kept_parts = [part[0]] + [swap(part[p], "tok", p) for p in range(1, toks)]

    norms, peak = block_norms(cand_parts, [hi - lo for lo, hi in bounds])
    peak = global_peak(peak)
    cand_score = (norms[:cand_share, 0] / (peak[0, 0] + 1e-06))[None]
    kept_grad = kept_sum(kept_parts)
    return (kept_grad, cand_score)


def solution(mesh):
    return jax.shard_map(
        local,
        mesh=mesh,
        in_specs=(P("tok", "blk"), P(("tok", "blk"), None), P(), P()),
        out_specs=(P("blk", "tok", None, None), P("blk", "tok")),
        check_vma=False,
    )
```

```python
import functools

import jax
import jax.numpy as jnp
from jax import lax
from jax.experimental import pallas as pl
from jax.experimental.pallas import tpu as pltpu
from jax.sharding import PartitionSpec as P

BLOCK = 128
ROWS = 16
PER_BLOCK = BLOCK // ROWS
VMEM_LIMIT = 40 * 1024 * 1024
ANY = pl.BlockSpec(memory_space=pl.ANY)
VMEM = pl.BlockSpec(memory_space=pltpu.VMEM)
SMEM = pl.BlockSpec(memory_space=pltpu.SMEM)
PARAMS = pltpu.CompilerParams(vmem_limit_bytes=VMEM_LIMIT)


def swap(x, axis, mask):
    size = lax.axis_size(axis)
    return lax.ppermute(x, axis, [(i, i ^ mask) for i in range(size)])


def call(kernel, outs, args, specs, out_specs, scratch=()):
    return pl.pallas_call(
        kernel,
        out_shape=outs,
        in_specs=specs,
        out_specs=out_specs,
        scratch_shapes=scratch,
        compiler_params=PARAMS,
    )(*args)


def pack_kernel(slots, masks, with_acts, pos, cols, grad, *refs):
    outs = refs[1:] if with_acts else refs
    me = pos[0]
    base = 0
    if with_acts:
        acts = refs[0]
        base = acts.shape[1] // ROWS
        for row in range(acts.shape[1] // BLOCK):
            block = acts[:, row * BLOCK : (row + 1) * BLOCK].T
            block = block.reshape(PER_BLOCK, ROWS, BLOCK)
            for out in outs:
                out[row * PER_BLOCK : (row + 1) * PER_BLOCK] = block
    for out, dests in zip(outs, masks):
        at = base
        for mask in dests:
            dest = me ^ mask
            for slot in slots:
                start = pl.multiple_of(cols[dest, slot] * BLOCK, BLOCK)
                out[at] = grad[:, pl.ds(start, BLOCK)]
                at += 1


def exchange(out_grad, cols, pos, slots, acts=None):
    owners = lax.axis_size("blk")
    masks = [(0,), (1,)] + [(m, m + 1) for m in range(2, owners, 2)]
    base = 0 if acts is None else acts.shape[1] // ROWS
    count = len(slots)
    buffers = call(
        functools.partial(pack_kernel, slots, masks, acts is not None),
        [
            jax.ShapeDtypeStruct((base + len(d) * count, ROWS, BLOCK), out_grad.dtype)
            for d in masks
        ],
        (pos, cols, out_grad) + (() if acts is None else (acts,)),
        [SMEM, SMEM, VMEM] + ([] if acts is None else [VMEM]),
        [VMEM] * len(masks),
    )
    got = [None] * owners
    got[0] = (buffers[0], base)
    for k in range(len(masks) - 1, 1, -1):
        got[2 * k - 2] = (swap(buffers[k], "blk", 2 * k - 2), base)
    got[1] = (swap(buffers[1], "blk", 1), base)
    for mask in range(2, owners, 2):
        got[mask + 1] = (swap(got[mask][0], "blk", 1), base + count)
    return got


def exchange_plain(out_grad, cols, pos, slots, acts=None):
    owners = lax.axis_size("blk")
    rows = out_grad.shape[0]
    count = len(slots)
    grad3 = out_grad.reshape(rows, -1, BLOCK)
    outgoing = jnp.take(grad3, cols[:, jnp.array(slots)].reshape(-1), axis=1)
    outgoing = outgoing.reshape(rows, owners, count, BLOCK).transpose(1, 2, 0, 3)
    incoming = lax.all_to_all(outgoing, "blk", 0, 0, tiled=True)
    grads = jnp.swapaxes(incoming, 0, 1).reshape(count * PER_BLOCK, ROWS, BLOCK)
    if acts is None:
        return [grads]
    whole = lax.all_gather(acts.T, "blk", axis=0, tiled=True)
    return [grads, whole.reshape(-1, ROWS, BLOCK)]


def product_kernel(plan, toks, share, first, pos, rows, *refs):
    copies_of, inputs = plan
    srcs = refs[:inputs]
    keep, send, acts_all, grad_all, sem = refs[inputs:]
    me, tok = pos[0], pos[1]
    copies = []
    for n, (which, src, begin, size, peer) in enumerate(copies_of):
        at = 0 if peer is None else me ^ peer
        from_ref = srcs[src].at[pl.ds(begin, size)]
        if which == "acts":
            dst = acts_all.at[pl.ds(pl.multiple_of(at * size, size), size)]
        elif peer is None:
            dst = grad_all
            from_ref = from_ref.reshape(grad_all.shape)
        else:
            dst = grad_all.at[:, pl.ds(pl.multiple_of(at * ROWS, ROWS), ROWS)]
        copies.append(pltpu.make_async_copy(from_ref, dst, sem.at[n]))
    for copy in copies:
        copy.start()
    for copy in copies:
        copy.wait()
    for peer in range(toks):
        unit = tok ^ peer
        for k in range(share):
            slot = unit * share + k
            row = rows[first(unit) + k] * PER_BLOCK
            left = acts_all[pl.ds(pl.multiple_of(row, PER_BLOCK), PER_BLOCK)]
            prod = jnp.dot(
                left.reshape(BLOCK, BLOCK), grad_all[slot], preferred_element_type=jnp.float32
            )
            out = send if peer % 2 else keep
            out[(peer // 2) * share + k] = prod.astype(out.dtype)


def products(acts_from, grads_from, width, rows, pos, toks, share, first, dtype):
    owners = lax.axis_size("blk")
    count = toks * share
    buffers = []
    copies = []

    def index(buffer):
        for n, other in enumerate(buffers):
            if other is buffer:
                return n
        buffers.append(buffer)
        return len(buffers) - 1

    if isinstance(acts_from[0], tuple):
        for peer in range(owners):
            copies.append(("acts", index(acts_from[peer][0]), 0, width, peer))
            buffer, begin = grads_from[peer]
            copies.append(("grad", index(buffer), begin, count, peer))
    else:
        whole = acts_from[1]
        copies.append(("acts", index(whole), 0, whole.shape[0], None))
        grads = grads_from[0]
        copies.append(("grad", index(grads), 0, grads.shape[0], None))
    units = toks // 2 * share
    return call(
        functools.partial(product_kernel, (copies, len(buffers)), toks, share, first),
        [
            jax.ShapeDtypeStruct((units, BLOCK, BLOCK), jnp.float32),
            jax.ShapeDtypeStruct((units, BLOCK, BLOCK), dtype),
        ],
        [pos, rows] + buffers,
        [SMEM, SMEM] + [ANY] * len(buffers),
        [VMEM] * 2,
        [
            pltpu.VMEM((owners * width, ROWS, BLOCK), jnp.bfloat16),
            pltpu.VMEM((count, BLOCK, BLOCK), jnp.bfloat16),
            pltpu.SemaphoreType.DMA((len(copies),)),
        ],
    )


def add_kernel(share, keep, got, keep_out, send_out):
    for k in range(keep.shape[0]):
        unit, part = divmod(k, share)
        total = keep[k] + got[k].astype(jnp.float32)
        out = send_out if unit % 2 else keep_out
        out[(unit // 2) * share + part] = total.astype(out.dtype)


def halve(keep, send, share):
    toks = lax.axis_size("tok")
    mask = 1
    got = swap(send, "tok", mask)
    while 2 * mask < toks:
        mask *= 2
        half = keep.shape[0] // 2
        keep, send = call(
            functools.partial(add_kernel, share),
            [
                jax.ShapeDtypeStruct((half, BLOCK, BLOCK), jnp.float32),
                jax.ShapeDtypeStruct((half, BLOCK, BLOCK), send.dtype),
            ],
            (keep, got),
            [VMEM] * 2,
            [VMEM] * 2,
        )
        got = swap(send, "tok", mask)
    return keep, got


def norm_kernel(*refs):
    row_out, peak_out = refs[-2:]
    lane = lax.broadcasted_iota(jnp.int32, row_out.shape, 1)
    row = jnp.zeros(row_out.shape, jnp.float32)
    at = 0
    for keep, got in zip(refs[:-2:2], refs[1:-2:2]):
        for k in range(keep.shape[0]):
            total = keep[k] + got[k].astype(jnp.float32)
            square = jnp.sum(jnp.sum(total * total, axis=0, keepdims=True), axis=1, keepdims=True)
            row = jnp.where(lane == at, square, row)
            at += 1
    norms = jnp.sqrt(row)
    row_out[...] = norms
    peak_out[...] = jnp.broadcast_to(jnp.max(norms, axis=1, keepdims=True), peak_out.shape)


def block_norms(pairs):
    shape = jax.ShapeDtypeStruct((8, BLOCK), jnp.float32)
    args = [x for pair in pairs for x in pair]
    return call(norm_kernel, [shape, shape], args, [VMEM] * len(args), [VMEM] * 2)


def peak_rounds():
    rounds = [("blk", [1])]
    for axis, low in (("blk", 2), ("tok", 1)):
        size = lax.axis_size(axis)
        while low < size:
            rounds.append((axis, [m for m in (low, 2 * low, 3 * low) if m < size]))
            low *= 4
    return rounds


def max_kernel(*refs):
    total = refs[0][...]
    for other in refs[1:-1]:
        total = jnp.maximum(total, other[...])
    refs[-1][...] = total


def score_kernel(row, *refs):
    peak = refs[0][...]
    for other in refs[1:-1]:
        peak = jnp.maximum(peak, other[...])
    out = refs[-1]
    score = row[...] / (peak + 1e-06)
    out[...] = score[0:1, 0 : out.shape[1]]


def scores(row, peak, count):
    rounds = peak_rounds()
    for n, (axis, masks) in enumerate(rounds):
        got = [peak] + [swap(peak, axis, m) for m in masks]
        if n < len(rounds) - 1:
            peak = functools.reduce(jnp.maximum, got)
    return call(
        score_kernel,
        jax.ShapeDtypeStruct((1, count), jnp.float32),
        [row] + got,
        [VMEM] * (1 + len(got)),
        VMEM,
    )


def kept_kernel(keep, got, out):
    out[0] = (keep[...] + got[...]).astype(out.dtype)


def local(acts, out_grad, kept_ids, cand_ids):
    toks = lax.axis_size("tok")
    me = lax.axis_index("blk")
    pos = jnp.stack([me, lax.axis_index("tok")]).astype(jnp.int32)
    ncols = out_grad.shape[1] // BLOCK
    ks = kept_ids.shape[1]
    kept_share, cand_share = ks // toks, cand_ids.shape[1] // toks
    ids = jnp.concatenate([kept_ids, cand_ids], axis=1)
    cols = ids % ncols
    rows = lax.dynamic_index_in_dim(ids, me, 0, keepdims=False) // ncols
    width = acts.shape[1] // ROWS
    move = exchange if out_grad.shape[0] % ROWS == 0 else exchange_plain

    half = cand_share // 2
    pairs = []
    acts_from = None
    for lo, hi in ((0, half), (half, cand_share)):
        slots = [ks + u * cand_share + k for u in range(toks) for k in range(lo, hi)]
        got = move(out_grad, cols, pos, slots, acts if acts_from is None else None)
        acts_from = acts_from or got
        first = lambda unit, lo=lo: ks + unit * cand_share + lo
        keep, send = products(
            acts_from, got, width, rows, pos, toks, hi - lo, first, jnp.bfloat16
        )
        pairs.append(halve(keep, send, hi - lo))
    got = move(out_grad, cols, pos, list(range(ks)))
    keep, send = products(
        acts_from, got, width, rows, pos, toks, kept_share, lambda u: u * kept_share, jnp.float32
    )
    kept_pair = halve(keep, send, kept_share)

    row, peak = block_norms(pairs)
    cand_score = scores(row, peak, cand_share)
    kept_grad = call(
        kept_kernel,
        jax.ShapeDtypeStruct((1, kept_share, BLOCK, BLOCK), jnp.bfloat16),
        kept_pair,
        [VMEM] * 2,
        VMEM,
    )
    return (kept_grad, cand_score)


def solution(mesh):
    return jax.shard_map(
        local,
        mesh=mesh,
        in_specs=(P("tok", "blk"), P(("tok", "blk"), None), P(), P()),
        out_specs=(P("blk", "tok", None, None), P("blk", "tok")),
        check_vma=False,
    )
```

```python
import functools

import jax
import jax.numpy as jnp
from jax import lax
from jax.experimental import pallas as pl
from jax.experimental.pallas import tpu as pltpu
from jax.sharding import PartitionSpec as P

BLOCK = 128
ROWS = 16
FIRST = 6
PER_BLOCK = BLOCK // ROWS
VMEM_LIMIT = 16 * 1024 * 1024
ANY = pl.BlockSpec(memory_space=pl.ANY)
VMEM = pl.BlockSpec(memory_space=pltpu.VMEM)
SMEM = pl.BlockSpec(memory_space=pltpu.SMEM)
COST = pl.CostEstimate(flops=1, bytes_accessed=1, transcendentals=0)
PARAMS = pltpu.CompilerParams(vmem_limit_bytes=VMEM_LIMIT)


def swap(x, axis, mask):
    size = lax.axis_size(axis)
    return lax.ppermute(x, axis, [(i, i ^ mask) for i in range(size)])


def after(x, *others):
    return lax.optimization_barrier((x, others))[0]


def call(kernel, outs, args, specs, out_specs, scratch=()):
    return pl.pallas_call(
        kernel,
        out_shape=outs,
        in_specs=specs,
        out_specs=out_specs,
        scratch_shapes=scratch,
        compiler_params=PARAMS,
        cost_estimate=COST,
    )(*args)


def pack_kernel(slots, masks, acts_width, extra, pos, cols, grad, *refs):
    me = pos[0]
    acts = refs[:1] if acts_width else ()
    others = refs[len(acts) : len(refs) - len(masks)]
    outs = refs[len(refs) - len(masks) :]
    for acts_ref in acts:
        for row in range(acts_width // BLOCK):
            block = acts_ref[:, row * BLOCK : (row + 1) * BLOCK].T
            block = block.reshape(PER_BLOCK, ROWS, BLOCK)
            for out in outs:
                out[row * PER_BLOCK : (row + 1) * PER_BLOCK] = block
    for out, dests in zip(outs, masks):
        at = acts_width // ROWS
        for mask in dests:
            dest = me ^ mask
            for slot in slots:
                start = pl.multiple_of(cols[dest, slot] * BLOCK, BLOCK)
                out[at] = grad[:, pl.ds(start, BLOCK)]
                at += 1
            for other in others:
                out[at : at + extra] = other[pl.ds(dest * extra, extra)]
                at += extra


def owner_masks():
    return [(0,), (1,)] + [(m, m + 1) for m in range(2, lax.axis_size("blk"), 2)]


def pack(out_grad, cols, pos, slots, acts=None, others=()):
    masks = owner_masks()
    width = 0 if acts is None else acts.shape[1]
    extra = others[0].shape[0] // lax.axis_size("blk") if others else 0
    count = len(slots) + extra * len(others)
    more = list(others) if acts is None else [acts]
    return call(
        functools.partial(pack_kernel, slots, masks, width, extra),
        [
            jax.ShapeDtypeStruct((width // ROWS + len(d) * count, ROWS, BLOCK), out_grad.dtype)
            for d in masks
        ],
        [pos, cols, out_grad] + more,
        [SMEM, SMEM] + [VMEM] * (1 + len(more)),
        [VMEM] * len(masks),
    )


def exchange(buffers):
    owners = lax.axis_size("blk")
    got = [None] * owners
    got[0] = buffers[0]
    for mask in range(owners - 2, 1, -2):
        got[mask] = swap(buffers[mask // 2 + 1], "blk", mask)
    got[1] = swap(buffers[1], "blk", 1)
    return got


def forward(got, count, *others):
    owners = len(got)
    base = got[0].shape[0] - count
    even = range(2, owners, 2)
    chips = after([got[m] for m in even], got[1], *others)
    for mask, buffer in zip(even, chips):
        got[mask] = buffer
        got[mask + 1] = swap(buffer, "blk", 1)
    return [(buffer, base + (count if m % 2 and m > 1 else 0)) for m, buffer in enumerate(got)]


def columns_plain(out_grad, cols, slots):
    owners = lax.axis_size("blk")
    rows = out_grad.shape[0]
    count = len(slots)
    grad3 = out_grad.reshape(rows, -1, BLOCK)
    outgoing = jnp.take(grad3, cols[:, jnp.array(slots)].reshape(-1), axis=1)
    outgoing = outgoing.reshape(rows, owners, count, BLOCK).transpose(1, 2, 0, 3)
    incoming = lax.all_to_all(outgoing, "blk", 0, 0, tiled=True)
    return jnp.swapaxes(incoming, 0, 1).reshape(count * PER_BLOCK, ROWS, BLOCK)


def kept_units(units, mask):
    return [unit for unit in units if not unit & mask]


def product_kernel(plan, toks, bounds, first, spare, pos, rows, *refs):
    copies_of, inputs = plan
    srcs = refs[:inputs]
    *outs, acts_all, grad_all, sem = refs[inputs:]
    keeps, sends = outs[: len(bounds)], outs[len(bounds) : 2 * len(bounds)]
    spares = outs[2 * len(bounds) :]
    share = bounds[-1][1]
    me, tok = pos[0], pos[1]
    copies = []
    for n, (which, src, begin, size, peer) in enumerate(copies_of):
        at = 0 if peer is None else me ^ peer
        from_ref = srcs[src].at[pl.ds(begin, size)]
        if which == "acts":
            dst = acts_all.at[pl.ds(pl.multiple_of(at * size, size), size)]
        elif peer is None:
            dst = grad_all
            from_ref = from_ref.reshape(grad_all.shape)
        else:
            dst = grad_all.at[:, pl.ds(pl.multiple_of(at * ROWS, ROWS), ROWS)]
        copies.append(pltpu.make_async_copy(from_ref, dst, sem.at[n]))
    for copy in copies:
        copy.start()
    for copy in copies:
        copy.wait()
    for peer in range(toks if spares else 0):
        for k in range(spare):
            row = rows[me, (tok ^ peer) * spare + k] * PER_BLOCK
            block = acts_all[pl.ds(pl.multiple_of(row, PER_BLOCK), PER_BLOCK)]
            spares[peer % 2][peer // 2 * spare + k] = block.reshape(BLOCK, BLOCK)
    for peer in range(toks):
        unit = tok ^ peer
        for k in range(share):
            slot = unit * share + k
            row = rows[me, first + slot] * PER_BLOCK
            left = acts_all[pl.ds(pl.multiple_of(row, PER_BLOCK), PER_BLOCK)]
            prod = jnp.dot(
                left.reshape(BLOCK, BLOCK), grad_all[slot], preferred_element_type=jnp.float32
            )
            for (lo, hi, mask), keep, send in zip(bounds, keeps, sends):
                if lo <= k < hi:
                    out = send if peer & mask else keep
                    at = kept_units(range(toks), mask).index(peer & ~mask)
                    out[at * (hi - lo) + k - lo] = prod.astype(out.dtype)


def gather_plan(owners, width, count, acts_from, grads_from):
    buffers = []
    copies = []

    def index(buffer):
        for n, other in enumerate(buffers):
            if other is buffer:
                return n
        buffers.append(buffer)
        return len(buffers) - 1

    if isinstance(acts_from, list):
        for peer in range(owners):
            copies.append(("acts", index(acts_from[peer][0]), 0, width, peer))
    elif acts_from is not None:
        copies.append(("acts", index(acts_from), 0, acts_from.shape[0], None))
    if isinstance(grads_from, list):
        for peer in range(owners):
            buffer, begin = grads_from[peer]
            copies.append(("grad", index(buffer), begin, count, peer))
    else:
        copies.append(("grad", index(grads_from), 0, grads_from.shape[0], None))
    return buffers, copies


def products(acts_from, grads_from, width, rows, pos, bounds, first, dtype, spare=0):
    owners, toks = lax.axis_size("blk"), lax.axis_size("tok")
    count = toks * bounds[-1][1]
    buffers, copies = gather_plan(owners, width, count, acts_from, grads_from)
    sizes = [toks // 2 * (hi - lo) for lo, hi, _ in bounds]
    spares = 2 if spare else 0
    return call(
        functools.partial(
            product_kernel, (copies, len(buffers)), toks, bounds, first, spare
        ),
        [jax.ShapeDtypeStruct((n, BLOCK, BLOCK), jnp.float32) for n in sizes]
        + [jax.ShapeDtypeStruct((n, BLOCK, BLOCK), dtype) for n in sizes]
        + [jax.ShapeDtypeStruct((toks // 2 * spare, BLOCK, BLOCK), jnp.bfloat16)] * spares,
        [pos, rows] + buffers,
        [SMEM, SMEM] + [ANY] * len(buffers),
        [VMEM] * (2 * len(bounds) + spares),
        [
            pltpu.VMEM((owners * width, ROWS, BLOCK), jnp.bfloat16),
            pltpu.VMEM((count, BLOCK, BLOCK), jnp.bfloat16),
            pltpu.SemaphoreType.DMA((len(copies),)),
        ],
    )


def kept_pack_kernel(share, pos, cols, grad, *outs):
    units = 2 * outs[0].shape[0] // share // cols.shape[0]
    for peer in range(units):
        unit = pos[1] ^ peer
        out = outs[peer % 2]
        for dest in range(cols.shape[0]):
            for k in range(share):
                start = pl.multiple_of(cols[dest, unit * share + k] * BLOCK, BLOCK)
                at = (dest * (units // 2) + peer // 2) * share + k
                out[at] = grad[:, pl.ds(start, BLOCK)]


def kept_pack(out_grad, cols, pos, share):
    owners, toks = lax.axis_size("blk"), lax.axis_size("tok")
    shape = (owners * (toks // 2) * share, ROWS, BLOCK)
    return call(
        functools.partial(kept_pack_kernel, share),
        [jax.ShapeDtypeStruct(shape, out_grad.dtype)] * 2,
        (pos, cols, out_grad),
        [SMEM, SMEM, VMEM],
        [VMEM] * 2,
    )


def kept_product_kernel(copies_of, inputs, share, pos, *refs):
    srcs = refs[:inputs]
    lefts = refs[inputs : inputs + 2]
    keep, send, grad_all, sem = refs[inputs + 2 :]
    copies = []
    for n, (_, src, begin, size, peer) in enumerate(copies_of):
        at = pl.multiple_of((pos[0] ^ peer) * ROWS, ROWS)
        copies.append(
            pltpu.make_async_copy(
                srcs[src].at[pl.ds(begin, size)], grad_all.at[:, pl.ds(at, ROWS)], sem.at[n]
            )
        )
    for copy in copies:
        copy.start()
    for copy in copies:
        copy.wait()
    half = lefts[0].shape[0]
    for k in range(half):
        total = jnp.zeros((BLOCK, BLOCK), jnp.float32)
        for part, left in enumerate(lefts):
            total += jnp.dot(
                left[k], grad_all[part * half + k], preferred_element_type=jnp.float32
            )
        unit, slot = divmod(k, share)
        (send if unit % 2 else keep)[unit // 2 * share + slot] = total


def kept_product(lefts, grads_from, pos, share):
    owners = lax.axis_size("blk")
    half = lefts[0].shape[0]
    buffers, copies = gather_plan(owners, 0, 2 * half, None, grads_from)
    return call(
        functools.partial(kept_product_kernel, copies, len(buffers), share),
        [jax.ShapeDtypeStruct((half // 2, BLOCK, BLOCK), jnp.float32)] * 2,
        [pos] + buffers + lefts,
        [SMEM] + [ANY] * len(buffers) + [VMEM] * 2,
        [VMEM] * 2,
        [
            pltpu.VMEM((2 * half, BLOCK, BLOCK), jnp.bfloat16),
            pltpu.SemaphoreType.DMA((len(copies),)),
        ],
    )


def add_kernel(share, units, mask, keep, got, keep_out, send_out):
    for at, unit in enumerate(kept_units(units, mask)):
        for out, source in ((keep_out, unit), (send_out, unit | mask)):
            begin = units.index(source) * share
            for k in range(share):
                total = keep[begin + k] + got[begin + k].astype(jnp.float32)
                out[at * share + k] = total.astype(out.dtype)


def add(keep, got, share, dtype, units, mask):
    half = keep.shape[0] // 2
    return call(
        functools.partial(add_kernel, share, units, mask),
        [
            jax.ShapeDtypeStruct((half, BLOCK, BLOCK), jnp.float32),
            jax.ShapeDtypeStruct((half, BLOCK, BLOCK), dtype),
        ],
        (keep, got),
        [VMEM] * 2,
        [VMEM] * 2,
    )


def halve(keep, send, share, masks, units=None):
    units = kept_units(units or range(lax.axis_size("tok")), masks[0])
    got = swap(send, "tok", masks[0])
    for mask in masks[1:]:
        keep, send = add(keep, got, share, send.dtype, units, mask)
        units = kept_units(units, mask)
        got = swap(send, "tok", mask)
    return keep, got


def norm_kernel(*refs):
    row_out, peak_out = refs[-2:]
    lane = lax.broadcasted_iota(jnp.int32, row_out.shape, 1)
    row = jnp.zeros(row_out.shape, jnp.float32)
    at = 0
    for keep, got in zip(refs[:-2:2], refs[1:-2:2]):
        for k in range(keep.shape[0]):
            total = keep[k] + got[k].astype(jnp.float32)
            square = jnp.sum(jnp.sum(total * total, axis=0, keepdims=True), axis=1, keepdims=True)
            row = jnp.where(lane == at, square, row)
            at += 1
    row = jnp.sqrt(row)
    row_out[...] = row
    peak_out[...] = jnp.broadcast_to(jnp.max(row[0:1], axis=1, keepdims=True), peak_out.shape)


def block_norms(*pairs):
    devices = lax.axis_size("tok") * lax.axis_size("blk")
    args = [x for pair in pairs for x in pair]
    return call(
        norm_kernel,
        [jax.ShapeDtypeStruct((n, BLOCK), jnp.float32) for n in (8, devices)],
        args,
        [VMEM] * len(args),
        [VMEM] * 2,
    )


def result_kernel(row, peaks, keep, got, kept, score):
    peak = jnp.max(peaks[...], axis=0, keepdims=True)
    score[...] = (row[0:1, :] / (peak + 1e-06))[:, 0 : score.shape[1]]
    kept[0] = (keep[...] + got[...]).astype(kept.dtype)


def results(row, peak, count, pair):
    peaks = lax.all_to_all(peak, ("tok", "blk"), 0, 0, tiled=True)
    return call(
        result_kernel,
        [
            jax.ShapeDtypeStruct((1,) + pair[0].shape, jnp.bfloat16),
            jax.ShapeDtypeStruct((1, count), jnp.float32),
        ],
        (row, peaks) + pair,
        [VMEM] * 4,
        [VMEM] * 2,
    )


def local(acts, out_grad, kept_ids, cand_ids):
    toks = lax.axis_size("tok")
    me = lax.axis_index("blk")
    pos = jnp.stack([me, lax.axis_index("tok")]).astype(jnp.int32)
    ncols = out_grad.shape[1] // BLOCK
    ks = kept_ids.shape[1]
    kept_share, cand_share = ks // toks, cand_ids.shape[1] // toks
    ids = jnp.concatenate([kept_ids, cand_ids], axis=1)
    cols = ids % ncols
    rows = ids // ncols
    width = acts.shape[1] // ROWS

    half = FIRST * cand_share // 12
    up = [1 << n for n in range(toks.bit_length() - 1)]
    orders = (up, up[::-1])
    bounds = ((0, half, orders[0][0]), (half, cand_share, orders[1][0]))
    cands = list(range(ks, ks + toks * cand_share))
    bf16, f32 = jnp.bfloat16, jnp.float32
    if out_grad.shape[0] % ROWS:
        whole = lax.all_gather(acts.T, "blk", axis=0, tiled=True).reshape(-1, ROWS, BLOCK)
        keep0, keep1, send0, send1 = products(
            whole, columns_plain(out_grad, cols, cands), width, rows, pos, bounds, ks, bf16
        )
        keep2, send2 = products(
            whole,
            columns_plain(out_grad, cols, list(range(ks))),
            width,
            rows,
            pos,
            ((0, kept_share, 1),),
            0,
            f32,
        )
        row, peak = block_norms(
            halve(keep0, send0, half, orders[0]), halve(keep1, send1, cand_share - half, orders[1])
        )
        pair2 = halve(keep2, send2, kept_share, up)
    else:
        buffers0 = pack(out_grad, cols, pos, cands, acts)
        cols = after(cols, buffers0[0])
        kept = kept_pack(out_grad, cols, pos, kept_share)
        arrived0 = exchange(buffers0)
        kept = [kept[0], swap(kept[1], "tok", 1)]
        buffers2 = pack(out_grad, cols, pos, [], None, kept)
        from0 = forward(arrived0, len(cands), buffers2[0])
        keep0, keep1, send0, send1, left, left_sent = products(
            from0, from0, width, rows, pos, bounds, ks, bf16, kept_share
        )
        arrived2 = exchange(after(buffers2, keep1))
        from2 = forward(arrived2, ks)
        lefts = [left, swap(left_sent, "tok", 1)]
        row, peak = block_norms(
            halve(keep0, send0, half, orders[0]),
            halve(after(keep1, *arrived2[2::2]), send1, cand_share - half, orders[1]),
        )
        keep2, send2 = kept_product(lefts, from2, pos, kept_share)
        pair2 = halve(keep2, after(send2, row), kept_share, up[1:], range(0, toks, 2))

    kept_grad, cand_score = results(row, peak, cand_share, pair2)
    return (kept_grad, cand_score)


def solution(mesh):
    return jax.shard_map(
        local,
        mesh=mesh,
        in_specs=(P("tok", "blk"), P(("tok", "blk"), None), P(), P()),
        out_specs=(P("blk", "tok", None, None), P("blk", "tok")),
        check_vma=False,
    )
```

```python
import functools

import jax
import jax.numpy as jnp
from jax import lax
from jax.experimental import pallas as pl
from jax.experimental.pallas import tpu as pltpu
from jax.sharding import PartitionSpec as P

BLOCK = 128
ROWS = 16
FIRST = 6
PER_BLOCK = BLOCK // ROWS
VMEM_LIMIT = 16 * 1024 * 1024
ANY = pl.BlockSpec(memory_space=pl.ANY)
VMEM = pl.BlockSpec(memory_space=pltpu.VMEM)
SMEM = pl.BlockSpec(memory_space=pltpu.SMEM)
COST = pl.CostEstimate(flops=1, bytes_accessed=1, transcendentals=0)
PARAMS = pltpu.CompilerParams(vmem_limit_bytes=VMEM_LIMIT)


def swap(x, axis, mask):
    size = lax.axis_size(axis)
    return lax.ppermute(x, axis, [(i, i ^ mask) for i in range(size)])


def after(x, *others):
    return lax.optimization_barrier((x, others))[0]


def call(kernel, outs, args, specs, out_specs, scratch=()):
    return pl.pallas_call(
        kernel,
        out_shape=outs,
        in_specs=specs,
        out_specs=out_specs,
        scratch_shapes=scratch,
        compiler_params=PARAMS,
        cost_estimate=COST,
    )(*args)


def pack_kernel(slots, masks, acts_width, pos, cols, grad, *refs):
    me = pos[0]
    acts, outs = refs[: -len(masks)], refs[-len(masks) :]
    for acts_ref in acts:
        for row in range(acts_width // BLOCK):
            block = acts_ref[:, row * BLOCK : (row + 1) * BLOCK].T
            block = block.reshape(PER_BLOCK, ROWS, BLOCK)
            for out in outs:
                out[row * PER_BLOCK : (row + 1) * PER_BLOCK] = block
    for out, dests in zip(outs, masks):
        at = acts_width // ROWS
        for mask in dests:
            dest = me ^ mask
            for slot in slots:
                start = pl.multiple_of(cols[dest, slot] * BLOCK, BLOCK)
                out[at] = grad[:, pl.ds(start, BLOCK)]
                at += 1


def owner_masks():
    return [(0,), (1,)] + [(m, m + 1) for m in range(2, lax.axis_size("blk"), 2)]


def pack(out_grad, cols, pos, slots, acts=None):
    masks = owner_masks()
    width = 0 if acts is None else acts.shape[1]
    return call(
        functools.partial(pack_kernel, slots, masks, width),
        [
            jax.ShapeDtypeStruct((width // ROWS + len(d) * len(slots), ROWS, BLOCK), out_grad.dtype)
            for d in masks
        ],
        [pos, cols, out_grad] + ([] if acts is None else [acts]),
        [SMEM, SMEM] + [VMEM] * (1 if acts is None else 2),
        [VMEM] * len(masks),
    )


def exchange(buffers):
    owners = lax.axis_size("blk")
    got = [None] * owners
    got[0] = buffers[0]
    for mask in range(owners - 2, 1, -2):
        got[mask] = swap(buffers[mask // 2 + 1], "blk", mask)
    got[1] = swap(buffers[1], "blk", 1)
    return got


def forward(got, count, *others):
    owners = len(got)
    base = got[0].shape[0] - count
    even = range(2, owners, 2)
    chips = after([got[m] for m in even], got[1], *others)
    for mask, buffer in zip(even, chips):
        got[mask] = buffer
        got[mask + 1] = swap(buffer, "blk", 1)
    return [(buffer, base + (count if m % 2 and m > 1 else 0)) for m, buffer in enumerate(got)]


def columns_plain(out_grad, cols, slots):
    owners = lax.axis_size("blk")
    rows = out_grad.shape[0]
    count = len(slots)
    grad3 = out_grad.reshape(rows, -1, BLOCK)
    outgoing = jnp.take(grad3, cols[:, jnp.array(slots)].reshape(-1), axis=1)
    outgoing = outgoing.reshape(rows, owners, count, BLOCK).transpose(1, 2, 0, 3)
    incoming = lax.all_to_all(outgoing, "blk", 0, 0, tiled=True)
    return jnp.swapaxes(incoming, 0, 1).reshape(count * PER_BLOCK, ROWS, BLOCK)


def kept_units(units, mask):
    return [unit for unit in units if not unit & mask]


def product_kernel(plan, toks, bounds, first, stride, pos, rows, *refs):
    copies_of, inputs = plan
    srcs = refs[:inputs]
    *outs, acts_all, grad_all, sem = refs[inputs:]
    keeps, sends = outs[: len(bounds)], outs[len(bounds) :]
    begin = bounds[0][0]
    share = bounds[-1][1] - begin
    me, tok = pos[0], pos[1]
    copies = []
    for n, (which, src, offset, size, peer) in enumerate(copies_of):
        at = 0 if peer is None else me ^ peer
        from_ref = srcs[src].at[pl.ds(offset, size)]
        if which == "acts":
            dst = acts_all.at[pl.ds(pl.multiple_of(at * size, size), size)]
        elif peer is None:
            dst = grad_all
            from_ref = from_ref.reshape(grad_all.shape)
        else:
            dst = grad_all.at[:, pl.ds(pl.multiple_of(at * ROWS, ROWS), ROWS)]
        copies.append(pltpu.make_async_copy(from_ref, dst, sem.at[n]))
    for copy in copies:
        copy.start()
    for copy in copies:
        copy.wait()
    for peer in range(toks):
        unit = tok ^ peer
        for k in range(share):
            slot = unit * share + k
            row = rows[me, first + unit * stride + begin + k] * PER_BLOCK
            left = acts_all[pl.ds(pl.multiple_of(row, PER_BLOCK), PER_BLOCK)]
            prod = jnp.dot(
                left.reshape(BLOCK, BLOCK), grad_all[slot], preferred_element_type=jnp.float32
            )
            for (lo, hi, mask), keep, send in zip(bounds, keeps, sends):
                if lo <= begin + k < hi:
                    out = send if peer & mask else keep
                    at = kept_units(range(toks), mask).index(peer & ~mask)
                    out[at * (hi - lo) + begin + k - lo] = prod.astype(out.dtype)


def gather_plan(owners, width, count, acts_from, grads_from):
    buffers = []
    copies = []

    def index(buffer):
        for n, other in enumerate(buffers):
            if other is buffer:
                return n
        buffers.append(buffer)
        return len(buffers) - 1

    if isinstance(acts_from, list):
        for peer in range(owners):
            copies.append(("acts", index(acts_from[peer][0]), 0, width, peer))
    elif acts_from is not None:
        copies.append(("acts", index(acts_from), 0, acts_from.shape[0], None))
    if isinstance(grads_from, list):
        for peer in range(owners):
            buffer, begin = grads_from[peer]
            copies.append(("grad", index(buffer), begin, count, peer))
    else:
        copies.append(("grad", index(grads_from), 0, grads_from.shape[0], None))
    return buffers, copies


def products(acts_from, grads_from, width, rows, pos, bounds, first, stride, dtype):
    owners, toks = lax.axis_size("blk"), lax.axis_size("tok")
    count = toks * (bounds[-1][1] - bounds[0][0])
    buffers, copies = gather_plan(owners, width, count, acts_from, grads_from)
    sizes = [toks // 2 * (hi - lo) for lo, hi, _ in bounds]
    return call(
        functools.partial(
            product_kernel, (copies, len(buffers)), toks, bounds, first, stride
        ),
        [jax.ShapeDtypeStruct((n, BLOCK, BLOCK), jnp.float32) for n in sizes]
        + [jax.ShapeDtypeStruct((n, BLOCK, BLOCK), dtype) for n in sizes],
        [pos, rows] + buffers,
        [SMEM, SMEM] + [ANY] * len(buffers),
        [VMEM] * (2 * len(bounds)),
        [
            pltpu.VMEM((owners * width, ROWS, BLOCK), jnp.bfloat16),
            pltpu.VMEM((count, BLOCK, BLOCK), jnp.bfloat16),
            pltpu.SemaphoreType.DMA((len(copies),)),
        ],
    )


def kept_pack_kernel(share, mask, width, pos, cols, grad, acts, own, other):
    half = own.shape[0] // share // cols.shape[0]
    other[:width] = acts[:width]
    for peer in range(2 * half):
        unit = pos[1] ^ peer
        index = kept_units(range(2 * half), mask).index(peer & ~mask)
        for dest in range(cols.shape[0]):
            at = (dest * half + index) * share
            out, at = (other, at + width) if peer & mask else (own, at)
            for k in range(share):
                start = pl.multiple_of(cols[dest, unit * share + k] * BLOCK, BLOCK)
                out[at + k] = grad[:, pl.ds(start, BLOCK)]


def kept_pack(out_grad, cols, pos, acts, width, share, mask):
    owners, toks = lax.axis_size("blk"), lax.axis_size("tok")
    count = owners * (toks // 2) * share
    return call(
        functools.partial(kept_pack_kernel, share, mask, width),
        [jax.ShapeDtypeStruct((n, ROWS, BLOCK), out_grad.dtype) for n in (count, width + count)],
        (pos, cols, out_grad, acts),
        [SMEM, SMEM, VMEM, VMEM],
        [VMEM] * 2,
    )


def kept_split_kernel(width, extra, masks, pos, own, other, *outs):
    for out, dests in zip(outs, masks):
        out[:width] = other[:width]
        at = width
        for mask in dests:
            dest = pos[0] ^ mask
            out[at : at + extra] = own[pl.ds(dest * extra, extra)]
            out[at + extra : at + 2 * extra] = other[pl.ds(width + dest * extra, extra)]
            at += 2 * extra


def kept_split(own, other, pos, width):
    masks = owner_masks()
    extra = own.shape[0] // lax.axis_size("blk")
    return call(
        functools.partial(kept_split_kernel, width, extra, masks),
        [
            jax.ShapeDtypeStruct((width + 2 * extra * len(d), ROWS, BLOCK), own.dtype)
            for d in masks
        ],
        (pos, own, other),
        [SMEM, VMEM, VMEM],
        [VMEM] * len(masks),
    )


def kept_product_kernel(copies_of, inputs, width, share, units, mask, pos, rows, *refs):
    srcs = refs[:inputs]
    keep, send, acts_all, grad_all, sem = refs[inputs:]
    me, tok = pos[0], pos[1]
    copies = []
    for n, (which, src, begin, size, peer) in enumerate(copies_of):
        if which == "grad":
            at = pl.multiple_of((me ^ peer) * ROWS, ROWS)
            dst = grad_all.at[:, pl.ds(at, ROWS)]
        else:
            at = pl.multiple_of((me ^ peer) * width, width)
            dst = acts_all.at[which, pl.ds(at, width)]
        copies.append(pltpu.make_async_copy(srcs[src].at[pl.ds(begin, size)], dst, sem.at[n]))
    for copy in copies:
        copy.start()
    for copy in copies:
        copy.wait()
    half = len(units) * share
    for index, unit in enumerate(units):
        out = send if unit & mask else keep
        at = kept_units(units, mask).index(unit & ~mask) * share
        for slot in range(share):
            row = rows[me, (tok ^ unit) * share + slot] * PER_BLOCK
            total = jnp.zeros((BLOCK, BLOCK), jnp.float32)
            for group in range(2):
                left = acts_all[group, pl.ds(pl.multiple_of(row, PER_BLOCK), PER_BLOCK)]
                total += jnp.dot(
                    left.reshape(BLOCK, BLOCK),
                    grad_all[group * half + index * share + slot],
                    preferred_element_type=jnp.float32,
                )
            out[at + slot] = total


def kept_product(from0, from2, rows, pos, width, share, units, mask):
    owners = lax.axis_size("blk")
    half = len(units) * share
    buffers = [buffer for buffer, _ in from0 + from2]
    copies = []
    for peer in range(owners):
        copies.append((0, peer, 0, width, peer))
        copies.append((1, owners + peer, 0, width, peer))
        copies.append(("grad", owners + peer, from2[peer][1], 2 * half, peer))
    return call(
        functools.partial(
            kept_product_kernel, copies, len(buffers), width, share, units, mask
        ),
        [jax.ShapeDtypeStruct((half // 2, BLOCK, BLOCK), jnp.float32)] * 2,
        [pos, rows] + buffers,
        [SMEM, SMEM] + [ANY] * len(buffers),
        [VMEM] * 2,
        [
            pltpu.VMEM((2, owners * width, ROWS, BLOCK), jnp.bfloat16),
            pltpu.VMEM((2 * half, BLOCK, BLOCK), jnp.bfloat16),
            pltpu.SemaphoreType.DMA((len(copies),)),
        ],
    )


def add_kernel(share, units, mask, keep, got, keep_out, send_out):
    for at, unit in enumerate(kept_units(units, mask)):
        for out, source in ((keep_out, unit), (send_out, unit | mask)):
            begin = units.index(source) * share
            for k in range(share):
                total = keep[begin + k] + got[begin + k].astype(jnp.float32)
                out[at * share + k] = total.astype(out.dtype)


def add(keep, got, share, dtype, units, mask):
    half = keep.shape[0] // 2
    return call(
        functools.partial(add_kernel, share, units, mask),
        [
            jax.ShapeDtypeStruct((half, BLOCK, BLOCK), jnp.float32),
            jax.ShapeDtypeStruct((half, BLOCK, BLOCK), dtype),
        ],
        (keep, got),
        [VMEM] * 2,
        [VMEM] * 2,
    )


def halve(keep, send, share, masks, units=None):
    units = kept_units(units or range(lax.axis_size("tok")), masks[0])
    got = swap(send, "tok", masks[0])
    for mask in masks[1:]:
        keep, send = add(keep, got, share, send.dtype, units, mask)
        units = kept_units(units, mask)
        got = swap(send, "tok", mask)
    return keep, got


def norm_kernel(*refs):
    row_out, peak_out = refs[-2:]
    lane = lax.broadcasted_iota(jnp.int32, row_out.shape, 1)
    row = jnp.zeros(row_out.shape, jnp.float32)
    at = 0
    for keep, got in zip(refs[:-2:2], refs[1:-2:2]):
        for k in range(keep.shape[0]):
            total = keep[k] + got[k].astype(jnp.float32)
            square = jnp.sum(jnp.sum(total * total, axis=0, keepdims=True), axis=1, keepdims=True)
            row = jnp.where(lane == at, square, row)
            at += 1
    row = jnp.sqrt(row)
    row_out[...] = row
    peak_out[...] = jnp.broadcast_to(jnp.max(row[0:1], axis=1, keepdims=True), peak_out.shape)


def block_norms(*pairs):
    devices = lax.axis_size("tok") * lax.axis_size("blk")
    args = [x for pair in pairs for x in pair]
    return call(
        norm_kernel,
        [jax.ShapeDtypeStruct((n, BLOCK), jnp.float32) for n in (8, devices)],
        args,
        [VMEM] * len(args),
        [VMEM] * 2,
    )


def result_kernel(row, peaks, keep, got, kept, score):
    peak = jnp.max(peaks[...], axis=0, keepdims=True)
    score[...] = (row[0:1, :] / (peak + 1e-06))[:, 0 : score.shape[1]]
    kept[0] = (keep[...] + got[...]).astype(kept.dtype)


def results(row, peak, count, pair):
    peaks = lax.all_to_all(peak, ("tok", "blk"), 0, 0, tiled=True)
    return call(
        result_kernel,
        [
            jax.ShapeDtypeStruct((1,) + pair[0].shape, jnp.bfloat16),
            jax.ShapeDtypeStruct((1, count), jnp.float32),
        ],
        (row, peaks) + pair,
        [VMEM] * 4,
        [VMEM] * 2,
    )


def local(acts, out_grad, kept_ids, cand_ids):
    toks = lax.axis_size("tok")
    me = lax.axis_index("blk")
    pos = jnp.stack([me, lax.axis_index("tok")]).astype(jnp.int32)
    ncols = out_grad.shape[1] // BLOCK
    ks = kept_ids.shape[1]
    kept_share, cand_share = ks // toks, cand_ids.shape[1] // toks
    ids = jnp.concatenate([kept_ids, cand_ids], axis=1)
    cols = ids % ncols
    rows = ids // ncols
    width = acts.shape[1] // ROWS

    half = FIRST * cand_share // 12
    up = [1 << n for n in range(toks.bit_length() - 1)]
    orders = (up, up[::-1])
    bounds = ((0, half, orders[0][0]), (half, cand_share, orders[1][0]))
    cands = list(range(ks, ks + toks * cand_share))
    bf16, f32 = jnp.bfloat16, jnp.float32
    if out_grad.shape[0] % ROWS:
        whole = lax.all_gather(acts.T, "blk", axis=0, tiled=True).reshape(-1, ROWS, BLOCK)
        keep0, keep1, send0, send1 = products(
            whole, columns_plain(out_grad, cols, cands), width, rows, pos, bounds, ks, cand_share, bf16
        )
        keep2, send2 = products(
            whole,
            columns_plain(out_grad, cols, list(range(ks))),
            width,
            rows,
            pos,
            ((0, kept_share, 1),),
            0,
            kept_share,
            f32,
        )
        row, peak = block_norms(
            halve(keep0, send0, half, orders[0]), halve(keep1, send1, cand_share - half, orders[1])
        )
        pair2 = halve(keep2, send2, kept_share, up)
    else:
        buffers0 = pack(out_grad, cols, pos, cands, acts)
        cols = after(cols, buffers0[0])
        own, other = kept_pack(out_grad, cols, pos, buffers0[0], width, kept_share, up[0])
        arrived0 = exchange(buffers0)
        buffers2 = kept_split(own, swap(other, 'tok', up[0]), pos, width)
        from0 = forward(arrived0, len(cands), buffers2[0])
        keep0, keep1, send0, send1 = products(from0, from0, width, rows, pos, bounds, ks, cand_share, bf16)
        units = [kept_units(range(toks), order[0]) for order in orders]
        step0 = swap(send0, 'tok', orders[0][0])
        step1 = swap(send1, 'tok', orders[1][0])
        arrived2 = exchange(buffers2)
        keep0, send0 = add(keep0, step0, half, bf16, units[0], orders[0][1])
        keep1 = after(keep1, send0)
        keep1, send1 = add(keep1, step1, cand_share - half, bf16, units[1], orders[1][1])
        from2 = forward(arrived2, ks)
        pair0 = halve(keep0, send0, half, orders[0][1:], units[0])
        pair1 = halve(keep1, send1, cand_share - half, orders[1][1:], units[1])
        from2[0] = (after(from2[0][0], send1), from2[0][1])
        evens = kept_units(range(toks), up[0])
        keep2, send2 = kept_product(from0, from2, rows, pos, width, kept_share, evens, up[1])
        row, peak = block_norms(pair0, pair1)
        send2 = after(send2, pair0[1], pair1[1])
        pair2 = halve(keep2, send2, kept_share, up[1:], range(0, toks, 2))

    kept_grad, cand_score = results(row, peak, cand_share, pair2)
    return (kept_grad, cand_score)


def solution(mesh):
    return jax.shard_map(
        local,
        mesh=mesh,
        in_specs=(P("tok", "blk"), P(("tok", "blk"), None), P(), P()),
        out_specs=(P("blk", "tok", None, None), P("blk", "tok")),
        check_vma=False,
    )
```
